32 devices in a mesh: row: 16 (over z, y, x), col: 2 (over core).
Axes of the slice: x: 2, y: 2, z: 4, core: 2. Of those that a mesh axis runs over, the one named last changes fastest.
Arguments:
- panel: bfloat16 [16384, 4096], P('row', 'col'), may hold values from -60 to 60, as said below
- sketch: bfloat16 [4096, 256], P('col'), may hold values from -0.09375 to 0.09375
Outputs:
- basis: float32 [16384, 256], P(('row', 'col'))
- upper: float32 [256, 256], replicated
The draws below stay inside these ranges and needn't reach their ends.
Inputs may be any that keep to these rules, and one draw needn't show every extreme that they name: `panel`: scaled expression values, real-valued, with scales that differ from cell to cell and from gene to gene.
All inputs are finite; a program needn't handle non-finite values.
Results may differ from the reference program's by a relative error of at most 0.0003.
Values sent between devices are 32-bit elements; how exact they have to be, the bound alone decides.
A program may use at most 64 MiB of HBM per device.

```python
import jax
import jax.numpy as jnp
from jax import lax

GP = 4096
S = 256
NROWS = 16384


def draw_panel(key, part):
    keys = jax.random.split(key, 3)
    values = jax.random.normal(keys[0], (NROWS, GP), jnp.float32)
    ramp = jnp.exp(jnp.log(3.0) * jnp.arange(NROWS, dtype=jnp.float32) / NROWS)
    row_scale = jnp.exp(jnp.log(10.0) * jax.random.uniform(keys[1], (NROWS, 1), jnp.float32)) * ramp[:, None] / 10.0
    col_scale = jnp.exp(jnp.log(10.0) * jax.random.uniform(keys[2], (1, GP), jnp.float32)) / 3.16
    return jnp.clip(values * row_scale * col_scale, -60.0, 60.0).astype(jnp.bfloat16)


def levels(stream_key, extent, cuts, low, high):
    level, own = 1.0, jax.random.fold_in(stream_key, 6)
    for axis_at, blocks in cuts:
        draws = jnp.exp(jax.random.uniform(jax.random.fold_in(own, axis_at), (blocks,), jnp.float32, low / len(cuts), high / len(cuts)))
        level = level * jnp.repeat(draws, extent[axis_at] // blocks).reshape([-1 if axis == axis_at else 1 for axis in range(len(extent))])
    return level


def gaussian(rng, shape, width, bound, shards=(), kind=jnp.bfloat16):
    values = width * jax.random.normal(rng, shape, jnp.float32)
    if shards:
        values = values * levels(rng, shape, shards, -0.22, 0.18)
    return jnp.clip(values, -bound, bound).astype(kind)


def setup_inputs(seed: int = 0) -> dict:
    streams_of = jax.random.split(jax.random.key(seed), 3)
    panel = draw_panel(jax.random.fold_in(streams_of[2], 71), 0)
    sketch = gaussian(streams_of[1], (GP, S), GP ** -0.5, 0.09375, ((0, 2),))
    return {"panel": panel, "sketch": sketch}


def reference(panel, sketch):
    sampled = jnp.dot(panel.astype(jnp.float32), sketch.astype(jnp.float32), preferred_element_type=jnp.float32)
    gram = jnp.dot(sampled.T, sampled, precision=lax.Precision.HIGHEST) / NROWS
    upper = jnp.linalg.cholesky(gram).T
    basis = jax.scipy.linalg.solve_triangular(upper.T, sampled.T, lower=True).T
    return (basis, upper)
```

```python
import functools

import jax
import jax.numpy as jnp
from jax import lax
from jax.experimental import pallas as pl
from jax.experimental.pallas import tpu as pltpu
from jax.sharding import PartitionSpec as P

MESH = pl.DeviceIdType.MESH
HIGHEST = lax.Precision.HIGHEST
MIB = 1 << 20
LANES = 128
SUB = 8
PANEL = 32
CHUNKS = 4


def radices(count):
    out = []
    while count > 1:
        for r in (4, 2, 3, 5, 7):
            if count % r == 0:
                break
        else:
            r = count
        out.append(r)
        count //= r
    return out


def plan(nrow, height):
    phases, stride = [], 1
    for r in radices(nrow):
        scatter = height % (SUB * r) == 0
        height = height // r if scatter else height
        phases.append((r, stride, height, scatter))
        stride *= r
    return phases


def tdot(a, b):
    return lax.dot_general(a, b, (((0,), (0,)), ((), ())), precision=HIGHEST, preferred_element_type=jnp.float32)


def sample_kernel(nrow, ncol, phases, total_rows, panel, sketch, block, gram, *scratch):
    (pan, sk, psend, precv, gsend, grecv, load_sem, sk_sem, ps_sem, pr_sem, gs_sem, gr_sem, ags_sem, agr_sem), rest = scratch[:14], scratch[14:]
    row, col = lax.axis_index("row"), lax.axis_index("col")
    share, size = block.shape
    height = size // ncol
    step = share // CHUNKS

    copy_sketch = pltpu.make_async_copy(sketch, sk, sk_sem)
    copy_sketch.start()
    loads = {}
    for d in list(range(1, ncol)) + [0]:
        owner = lax.rem(col + d, ncol)
        for c in range(CHUNKS):
            at = pl.ds(pl.multiple_of(owner * share + c * step, step), step)
            loads[d, c] = pltpu.make_async_copy(panel.at[at, :], pan.at[pl.ds((d * CHUNKS + c) * step, step), :], load_sem.at[d * CHUNKS + c])
            loads[d, c].start()

    barrier = pltpu.get_barrier_semaphore()
    count = 0
    for d in range(1, ncol):
        pl.semaphore_signal(barrier, inc=1, device_id=(row, lax.rem(col + d, ncol)), device_id_type=MESH)
        count += 1
    peers = []
    for r, stride, _, _ in phases:
        digit = lax.rem(row // stride, r)
        mine = []
        for d in range(1, r):
            other = lax.rem(digit + d, r)
            target = (row + (other - digit) * stride, col)
            mine.append((other, target))
            pl.semaphore_signal(barrier, inc=1, device_id=target, device_id_type=MESH)
            count += 1
        peers.append((digit, mine))

    sends, arrivals = [], []
    copy_sketch.wait()
    first = True
    for d in range(1, ncol):
        owner = lax.rem(col + d, ncol)
        for c in range(CHUNKS):
            loads[d, c].wait()
            at = pl.ds((d - 1) * share + c * step, step)
            psend[at, :] = jnp.dot(pan[pl.ds((d * CHUNKS + c) * step, step), :], sk[...], preferred_element_type=jnp.float32)
            if first:
                pl.semaphore_wait(barrier, count)
                first = False
            k = (d - 1) * CHUNKS + c
            copy = pltpu.make_async_remote_copy(psend.at[at, :], precv.at[at, :], ps_sem.at[k], pr_sem.at[k], device_id=(row, owner), device_id_type=MESH)
            copy.start()
            sends.append(copy)
            arrivals.append((copy, at, c))
    for c in range(CHUNKS):
        loads[0, c].wait()
        block[pl.ds(c * step, step), :] = jnp.dot(pan[pl.ds(c * step, step), :], sk[...], preferred_element_type=jnp.float32)
    for copy, at, c in arrivals:
        copy.wait_recv()
        own = pl.ds(c * step, step)
        block[own, :] = block[own, :] + precv[at, :]

    arrivals = []
    for d in range(1, ncol):
        owner = lax.rem(col + d, ncol)
        cols = pl.ds(pl.multiple_of(owner * height, height), height)
        gsend[d - 1] = tdot(block[:, cols], block[...])
        copy = pltpu.make_async_remote_copy(gsend.at[d - 1], grecv.at[d - 1], gs_sem.at[d - 1], gr_sem.at[d - 1], device_id=(row, owner), device_id_type=MESH)
        copy.start()
        sends.append(copy)
        arrivals.append(copy)
    cols = pl.ds(pl.multiple_of(col * height, height), height)
    value = tdot(block[:, cols], block[...])
    for d, copy in enumerate(arrivals):
        copy.wait_recv()
        value = value + grecv[d]

    base = col * height
    bases = []
    for i, (r, stride, rows, scatter) in enumerate(phases):
        acc, buf, s_sem, r_sem = rest[4 * i : 4 * i + 4]
        digit, mine = peers[i]
        acc[...] = value
        arrivals = []
        for d, (other, target) in enumerate(mine):
            if scatter:
                src, dst = acc.at[pl.ds(pl.multiple_of(other * rows, rows), rows), :], buf.at[d]
            else:
                src, dst = acc, buf.at[digit]
            copy = pltpu.make_async_remote_copy(src, dst, s_sem.at[d], r_sem.at[d], device_id=target, device_id_type=MESH)
            copy.start()
            sends.append(copy)
            arrivals.append(copy)
        if scatter:
            base = base + digit * rows
            value = acc[pl.ds(pl.multiple_of(digit * rows, rows), rows), :]
            for d, copy in enumerate(arrivals):
                copy.wait_recv()
                value = value + buf[d]
        else:
            buf[digit] = acc[...]
            for copy in arrivals:
                copy.wait_recv()
            value = buf[0]
            for d in range(1, r):
                value = value + buf[d]
        bases.append(base)
    rows = phases[-1][2] if phases else height
    gram[pl.ds(pl.multiple_of(base, rows), rows), :] = value / total_rows

    for i in reversed(range(len(phases))):
        r, stride, rows, scatter = phases[i]
        if not scatter:
            continue
        s_sem, r_sem = rest[4 * i + 2 : 4 * i + 4]
        digit, mine = peers[i]
        at = pl.ds(pl.multiple_of(bases[i], rows), rows)
        arrivals = []
        for d, (other, target) in enumerate(mine):
            copy = pltpu.make_async_remote_copy(gram.at[at, :], gram.at[at, :], s_sem.at[r - 1 + d], r_sem.at[r - 1 + d], device_id=target, device_id_type=MESH)
            copy.start()
            sends.append(copy)
            arrivals.append(copy)
        for copy in arrivals:
            copy.wait_recv()
    arrivals = []
    at = pl.ds(pl.multiple_of(col * height, height), height)
    for d in range(1, ncol):
        copy = pltpu.make_async_remote_copy(gram.at[at, :], gram.at[at, :], ags_sem.at[d - 1], agr_sem.at[d - 1], device_id=(row, lax.rem(col + d, ncol)), device_id_type=MESH)
        copy.start()
        sends.append(copy)
        arrivals.append(copy)
    for copy in arrivals:
        copy.wait_recv()
    for copy in sends:
        copy.wait_send()


def spread(x, at):
    return jnp.broadcast_to(x[at : at + 1, :], x.shape)


def split(x):
    hi = x.astype(jnp.bfloat16)
    left = x - hi.astype(jnp.float32)
    mid = left.astype(jnp.bfloat16)
    return hi, mid, (left - mid.astype(jnp.float32)).astype(jnp.bfloat16)


def recip(d):
    r = pl.reciprocal(d, approx=True)
    r = r * (2.0 - d * r)
    return r * (2.0 - d * r)


def factor_kernel(gram, block, basis, upper, work, inverse):
    size = gram.shape[0]
    tiles = size // LANES
    groups = PANEL // SUB
    sub = lax.broadcasted_iota(jnp.int32, (SUB, LANES), 0)
    lane = lax.broadcasted_iota(jnp.int32, (SUB, LANES), 1)
    work[...] = gram[...]
    rows_of = lax.broadcasted_iota(jnp.int32, (size, size), 0)
    cols_of = lax.broadcasted_iota(jnp.int32, (size, size), 1)
    inverse[...] = jnp.where(rows_of == cols_of, 1.0, 0.0)
    upper[...] = jnp.zeros_like(upper)
    for low in range(0, size, PANEL):
        first = low // LANES
        kinds = [(work, t) for t in range(first, tiles)] + [(inverse, t) for t in range(first + 1)]
        part = [[ref[low + SUB * g : low + SUB * (g + 1), LANES * t : LANES * (t + 1)] for ref, t in kinds] for g in range(groups)]
        off = low % LANES
        column = {}
        for q in range(PANEL):
            for g in range(q // SUB, groups):
                column[q, g] = jnp.broadcast_to(part[g][0][:, off + q : off + q + 1], (SUB, LANES))
        diagonal = [jnp.ones((SUB, LANES), jnp.float32) for _ in range(groups)]
        for p in range(PANEL):
            gp, sp = divmod(p, SUB)
            pivot = spread(column[p, gp], sp)
            diagonal[gp] = jnp.where(sub == sp, pivot, diagonal[gp])
            inv = recip(pivot)
            weight = {g: column[p, g] * inv for g in range(gp, groups)}
            for q in range(p + 1, PANEL):
                value = spread(column[p, q // SUB], q % SUB)
                for g in range(q // SUB, groups):
                    column[q, g] = column[q, g] - weight[g] * value
            weight[gp] = jnp.where(sub > sp, weight[gp], 0.0)
            for x in range(len(kinds)):
                value = spread(part[gp][x], sp)
                for g in range(gp, groups):
                    part[g][x] = part[g][x] - weight[g] * value
        for g in range(groups):
            scale = lax.rsqrt(diagonal[g])
            at = slice(low + SUB * g, low + SUB * (g + 1))
            for x, (ref, t) in enumerate(kinds):
                part[g][x] = part[g][x] * scale
                where = slice(LANES * t, LANES * (t + 1))
                if ref is work:
                    upper[at, where] = jnp.where(lane + LANES * t >= sub + (low + SUB * g), part[g][x], 0.0)
                else:
                    inverse[at, where] = part[g][x]
        if low + PANEL < size:
            wide = (tiles - first) * LANES
            rows = jnp.concatenate([jnp.concatenate(part[g], axis=1) for g in range(groups)], axis=0)
            hi, mid, lo = split(rows)
            left = jnp.concatenate([x[:, :wide] for x in (hi, hi, mid, hi, lo, mid)], axis=0)
            right = jnp.concatenate([hi, mid, hi, lo, hi, mid], axis=0)
            change = lax.dot_general(left, right, (((0,), (0,)), ((), ())), preferred_element_type=jnp.float32)
            skip = low + PANEL - first * LANES
            work[low + PANEL :, first * LANES :] = work[low + PANEL :, first * LANES :] - change[skip:, :wide]
            inverse[low + PANEL :, : (first + 1) * LANES] = inverse[low + PANEL :, : (first + 1) * LANES] - change[skip:, wide:]
    basis[...] = lax.dot_general(block[...], inverse[...], (((1,), (1,)), ((), ())), precision=HIGHEST, preferred_element_type=jnp.float32)


def local(panel, sketch):
    rows, depth = panel.shape
    size = sketch.shape[1]
    ncol, nrow = lax.axis_size("col"), lax.axis_size("row")
    share, height = rows // ncol, size // ncol
    phases = plan(nrow, height)
    f32 = jnp.float32
    dma = pltpu.SemaphoreType.DMA
    vmem = pl.BlockSpec(memory_space=pltpu.VMEM)
    anywhere = pl.BlockSpec(memory_space=pl.ANY)
    others = max(ncol - 1, 1)
    scratch = [
        pltpu.VMEM((rows, depth), panel.dtype),
        pltpu.VMEM((depth, size), sketch.dtype),
        pltpu.VMEM((others * share, size), f32),
        pltpu.VMEM((others * share, size), f32),
        pltpu.VMEM((others, height, size), f32),
        pltpu.VMEM((others, height, size), f32),
        dma((ncol * CHUNKS,)),
        dma,
        dma((others * CHUNKS,)),
        dma((others * CHUNKS,)),
        dma((others,)),
        dma((others,)),
        dma((others,)),
        dma((others,)),
    ]
    tall = height
    for r, _, piece, scatter in phases:
        scratch += [
            pltpu.VMEM((tall, size), f32),
            pltpu.VMEM((r - 1 if scatter else r, piece, size), f32),
            dma((2 * (r - 1),)),
            dma((2 * (r - 1),)),
        ]
        tall = piece
    block, gram = pl.pallas_call(
        functools.partial(sample_kernel, nrow, ncol, phases, float(rows * nrow)),
        out_shape=(jax.ShapeDtypeStruct((share, size), f32), jax.ShapeDtypeStruct((size, size), f32)),
        in_specs=[anywhere, anywhere],
        out_specs=(vmem, vmem),
        scratch_shapes=scratch,
        compiler_params=pltpu.CompilerParams(collective_id=0, has_side_effects=True, vmem_limit_bytes=32 * MIB),
        cost_estimate=pl.CostEstimate(flops=2 * rows * depth * size, bytes_accessed=2 * (rows + size) * depth, transcendentals=0),
        name="sample",
    )(panel, sketch)
    return pl.pallas_call(
        factor_kernel,
        out_shape=(jax.ShapeDtypeStruct((share, size), f32), jax.ShapeDtypeStruct((size, size), f32)),
        in_specs=[vmem, vmem],
        out_specs=(vmem, vmem),
        scratch_shapes=[pltpu.VMEM((size, size), f32), pltpu.VMEM((size, size), f32)],
        compiler_params=pltpu.CompilerParams(vmem_limit_bytes=32 * MIB),
        cost_estimate=pl.CostEstimate(flops=2 * share * size * size, bytes_accessed=8 * (share + size) * size, transcendentals=0),
        name="factor",
    )(gram, block)


def solution(mesh):
    return jax.shard_map(
        local,
        mesh=mesh,
        in_specs=(P("row", "col"), P("col", None)),
        out_specs=(P(("row", "col"), None), P()),
        check_vma=False,
    )
```
